32 devices in a mesh: groups: 2 (over y), pool: 4 (over z), tp: 2 (over x), kvrep: 2 (over core).
Axes of the slice: x: 2, y: 2, z: 4, core: 2. Of those that a mesh axis runs over, the one named last changes fastest.
Arguments:
- queries: bfloat16 [1792, 64, 128], P(('groups', 'pool', 'kvrep'), 'tp'), parts along dimension 0, may hold values from -120 to 120
- new_keys: bfloat16 [1792, 8, 128], P(('groups', 'pool', 'kvrep'), 'tp'), parts along dimension 0, may hold values from -4 to 4
- suffix_values: bfloat16 [1792, 8, 128], P(('groups', 'pool', 'kvrep'), 'tp'), parts along dimension 0, may hold values from -4 to 4
- pool_key_values: bfloat16 [128, 2, 8, 256, 128], P(('groups', 'pool'), None, 'tp'), parts along dimension 0, may hold values from -4 to 4
- block_slots: int32 [8, 4, 8], P('groups'), parts along dimension 0, may hold values from 0 to 15, as said below
- counts: int32 [8, 4], P('groups'), parts along dimension 0, may hold values from 0 to 8, as said below
- slot_fill: int32 [128], P('groups'), parts along dimension 0, may hold values from 1 to 256, as said below
Outputs:
- attended: bfloat16 [1792, 64, 128], P(('groups', 'pool', 'kvrep'), 'tp'), parts along dimension 0
The draws below stay inside these ranges and needn't reach their ends.
There are 2 independent parts, one for each index of `groups`. The reference program is written for one: setup_inputs(seed, part) draws one part's arguments, and reference() takes and returns one part's arrays. A program takes and returns all parts, laid end to end along the dimension named above; each array names one. Nothing has to cross between parts.
Inputs may be any that keep to these rules, and one draw needn't show every extreme that they name: block_slots[o, d, k] for k < counts[o, d] are distinct over all d and k of one owner o; the entries past counts are slots of the same owner too. Every owner's counts sum to 16; one document has 8 blocks on every owner. `slot_fill`: the filled token slots of a block are its first ones.
All inputs are finite; a program needn't handle non-finite values.
Results may differ from the reference program's by a relative error of at most 0.0031.
Values may be sent and summed in bfloat16 or wider, within the bound.
A program may use at most 128 MiB of HBM per device.

```python
import math
import jax
import jax.numpy as jnp
from jax import lax

QUERY_HEADS = 64
KEY_VALUE_HEADS = 8
HEAD_SIZE = 128
BLOCK_TOKENS = 256
BLK_DEV = 16
CAP = 8
SUFFIX_TOKENS = 224
TOKENS_TOTAL = 896
POOL_BLOCKS = 64
N_POOL = 4


def shared_draw(key):
    base_offset = jnp.clip(jax.random.normal(jax.random.fold_in(key, 21), (TOKENS_TOTAL, KEY_VALUE_HEADS, HEAD_SIZE), jnp.float32), -4.0, 4.0)
    return base_offset


def layout_tables(key):
    owner_keys = jax.random.split(jax.random.fold_in(key, 31), N_POOL)
    longest = jax.random.randint(jax.random.fold_in(key, 32), (), 0, N_POOL)
    doc_index = jnp.arange(N_POOL, dtype=jnp.int32)

    def one_owner(owner_key):
        pick_key, order_key = jax.random.split(owner_key)
        ordering = jax.random.permutation(pick_key, (N_POOL - 1) * CAP)
        chosen = (ordering < BLK_DEV - CAP).astype(jnp.int32).reshape(N_POOL - 1, CAP)
        others = jnp.sum(chosen, axis=1)
        other_index = jnp.clip(doc_index - (doc_index > longest).astype(jnp.int32), 0, N_POOL - 2)
        held_count = jnp.where(doc_index == longest, CAP, others[other_index]).astype(jnp.int32)
        offsets = jnp.cumsum(held_count) - held_count
        shuffled = jax.random.permutation(order_key, BLK_DEV)
        position = (offsets[:, None] + jnp.arange(CAP, dtype=jnp.int32)[None, :]) % BLK_DEV
        return (shuffled[position].astype(jnp.int32), held_count)
    return jax.vmap(one_owner)(owner_keys)


def draw_queries(key, part):
    key = jax.random.fold_in(key, 5)
    drawn = 2.5 * jnp.clip(jax.random.normal(key, (TOKENS_TOTAL, QUERY_HEADS, HEAD_SIZE), jnp.float32), -4.0, 4.0)
    return drawn.astype(jnp.bfloat16)


def draw_new_keys(key, part):
    base_offset = shared_draw(key)
    return base_offset.astype(jnp.bfloat16)


def draw_block_slots(key, part):
    slots_table, held_table = layout_tables(key)
    return slots_table


def draw_counts(key, part):
    slots_table, held_table = layout_tables(key)
    return held_table


def draw_slot_fill(key, part):
    key = jax.random.fold_in(key, 3)
    partial_key, value_key = jax.random.split(key)
    partial_value = jax.random.randint(partial_key, (POOL_BLOCKS,), 0, 4) == 0
    amount = jax.random.randint(value_key, (POOL_BLOCKS,), 1, BLOCK_TOKENS + 1)
    return jnp.where(partial_value, amount, BLOCK_TOKENS).astype(jnp.int32)


def levels(key, dims, pieces, least, high):
    factor_of, own = 1.0, jax.random.fold_in(key, 6)
    for dim, shards_of in pieces:
        heights = jnp.exp(jax.random.uniform(jax.random.fold_in(own, dim), (shards_of,), jnp.float32, least / len(pieces), high / len(pieces)))
        factor_of = factor_of * jnp.repeat(heights, dims[dim] // shards_of).reshape([-1 if axis == dim else 1 for axis in range(len(dims))])
    return factor_of


def bell_draw(key, dims, deviation, limit, cuts=(), held_as=jnp.bfloat16):
    array = deviation * jax.random.normal(key, dims, jnp.float32)
    if cuts:
        array = array * levels(key, dims, cuts, -0.22, 0.18)
    return jnp.clip(array, -limit, limit).astype(held_as)


def setup_inputs(seed: int = 0, part: int = 0) -> dict:
    seeds = jax.random.split(jax.random.key(seed), 8)
    own_keys = jax.random.split(jax.random.fold_in(seeds[7], part), 8)
    return {
        "queries": draw_queries(jax.random.fold_in(jax.random.fold_in(seeds[7], part), 71), part),
        "new_keys": draw_new_keys(jax.random.fold_in(jax.random.fold_in(seeds[7], part), 71), part),
        "suffix_values": bell_draw(own_keys[2], (TOKENS_TOTAL, KEY_VALUE_HEADS, HEAD_SIZE), 1.0, 4.0, ((0, 8), (1, 2))),
        "pool_key_values": bell_draw(own_keys[3], (POOL_BLOCKS, 2, KEY_VALUE_HEADS, BLOCK_TOKENS, HEAD_SIZE), 1.0, 4.0, ((0, 4), (2, 2))),
        "block_slots": draw_block_slots(jax.random.fold_in(jax.random.fold_in(seeds[7], part), 71), part),
        "counts": draw_counts(jax.random.fold_in(jax.random.fold_in(seeds[7], part), 71), part),
        "slot_fill": draw_slot_fill(jax.random.fold_in(jax.random.fold_in(seeds[7], part), 71), part),
    }


def reference(queries, new_keys, suffix_values, pool_key_values, block_slots, counts, slot_fill):
    query_group_size = QUERY_HEADS // KEY_VALUE_HEADS
    factor = 1.0 / math.sqrt(HEAD_SIZE)
    owner_base = jnp.arange(N_POOL, dtype=jnp.int32)[:, None] * BLK_DEV
    rank_index = jnp.arange(CAP, dtype=jnp.int32)
    block_token = jnp.arange(BLOCK_TOKENS, dtype=jnp.int32)
    suffix_pos = jnp.arange(SUFFIX_TOKENS, dtype=jnp.int32)
    causal = jnp.repeat(suffix_pos[None, :] <= suffix_pos[:, None], query_group_size, axis=0)

    def one_document(document):
        flat_index = (owner_base + block_slots[:, document, :]).astype(jnp.int32)
        filled = slot_fill[flat_index]
        held_count = counts[:, document]
        usable = (rank_index[None, :, None] < held_count[:, None, None]) & (block_token[None, None, :] < filled[:, :, None])
        usable = usable.reshape(-1)
        prefix = pool_key_values[flat_index.reshape(-1)]
        first_row = (document * SUFFIX_TOKENS).astype(jnp.int32)
        doc_queries = lax.dynamic_slice_in_dim(queries, first_row, SUFFIX_TOKENS, 0)
        doc_keys = lax.dynamic_slice_in_dim(new_keys, first_row, SUFFIX_TOKENS, 0)
        doc_values = lax.dynamic_slice_in_dim(suffix_values, first_row, SUFFIX_TOKENS, 0)
        allowed = jnp.concatenate([jnp.broadcast_to(usable[None, :], (SUFFIX_TOKENS * query_group_size, usable.shape[0])), causal], axis=1)

        def single_head(head):
            key_rows = jnp.concatenate([prefix[:, 0, head].reshape(-1, HEAD_SIZE), doc_keys[:, head]], axis=0)
            value_rows = jnp.concatenate([prefix[:, 1, head].reshape(-1, HEAD_SIZE), doc_values[:, head]], axis=0)
            query_rows = lax.dynamic_slice_in_dim(doc_queries, (head * query_group_size).astype(jnp.int32), query_group_size, 1).reshape(SUFFIX_TOKENS * query_group_size, HEAD_SIZE)
            scores = jnp.dot(query_rows, key_rows.T, preferred_element_type=jnp.float32) * factor
            masked = jnp.where(allowed, scores, -1e+30)
            highest = lax.optimization_barrier(jnp.max(masked, axis=1, keepdims=True))
            weights = jnp.where(allowed, jnp.exp(masked - highest), 0.0)
            denominator = lax.optimization_barrier(jnp.sum(weights, axis=1, keepdims=True))
            summed = jnp.dot(weights.astype(jnp.bfloat16), value_rows, preferred_element_type=jnp.float32)
            return (summed / denominator).astype(jnp.bfloat16)
        head_outputs = lax.map(single_head, jnp.arange(KEY_VALUE_HEADS, dtype=jnp.int32))
        return head_outputs.reshape(KEY_VALUE_HEADS, SUFFIX_TOKENS, query_group_size, HEAD_SIZE).transpose(1, 0, 2, 3).reshape(SUFFIX_TOKENS, QUERY_HEADS, HEAD_SIZE)
    documents = lax.map(one_document, jnp.arange(N_POOL, dtype=jnp.int32))
    return documents.reshape(TOKENS_TOTAL, QUERY_HEADS, HEAD_SIZE)
```

```python
import functools
import math

import jax
import jax.numpy as jnp
from jax import lax
from jax.experimental import pallas as pl
from jax.experimental.pallas import tpu as pltpu
from jax.sharding import PartitionSpec as P

negative = -1e30
NT = (((1,), (1,)), ((), ()))
TN = (((0,), (0,)), ((), ()))


def attend_step(state, key_rows, value_rows, query_rows, scale, allowed):
    highest, total, summed = state
    scores = lax.dot_general(key_rows, query_rows, NT, preferred_element_type=jnp.float32)
    if allowed is not None:
        scores = jnp.where(allowed, scores, negative)
    peak = jnp.maximum(highest, jnp.max(scores, axis=0, keepdims=True))
    weights = jnp.exp2((scores - peak) * scale)
    if allowed is not None:
        weights = jnp.where(allowed, weights, 0.0)
    decay = jnp.exp2((highest - peak) * scale)
    total = total * decay + jnp.sum(weights, axis=0, keepdims=True)
    product = lax.dot_general(
        value_rows, weights.astype(jnp.bfloat16), TN, preferred_element_type=jnp.float32
    )
    return peak, total, summed * decay + product


def attend_kernel(
    scale, group, place_ref, counts_ref, slots_ref, fill_ref,
    query_ref, pool_ref, keys_ref, values_ref, out_ref, log_ref,
    highest_ref, total_ref, summed_ref,
):
    head, document = pl.program_id(0), pl.program_id(1)
    position, replica = place_ref[0], place_ref[1]
    query_rows = query_ref[0, 0]
    rows = query_rows.shape[0]
    highest_ref[...] = jnp.full_like(highest_ref, negative)
    total_ref[...] = jnp.zeros_like(total_ref)
    summed_ref[...] = jnp.zeros_like(summed_ref)

    def advance(key_rows, value_rows, allowed):
        state = highest_ref[...], total_ref[...], summed_ref[...]
        state = attend_step(state, key_rows, value_rows, query_rows, scale, allowed)
        highest_ref[...], total_ref[...], summed_ref[...] = state

    @pl.when(document == position)
    def _():
        key_rows, value_rows = keys_ref[0], values_ref[0]
        shape = (key_rows.shape[0], rows)
        query_pos = replica * (rows // group) + lax.broadcasted_iota(jnp.int32, shape, 1) // group
        advance(key_rows, value_rows, lax.broadcasted_iota(jnp.int32, shape, 0) <= query_pos)

    def one_block(rank, _):
        slot = slots_ref[document, rank]
        filled = fill_ref[slot]
        key_rows, value_rows = pool_ref[slot, 0, 0], pool_ref[slot, 1, 0]

        @pl.when(filled >= key_rows.shape[0])
        def _():
            advance(key_rows, value_rows, None)

        @pl.when(filled < key_rows.shape[0])
        def _():
            shape = (key_rows.shape[0], rows)
            advance(key_rows, value_rows, lax.broadcasted_iota(jnp.int32, shape, 0) < filled)

        return 0

    lax.fori_loop(0, counts_ref[document], one_block, 0)
    total = total_ref[...]
    held = total > 0.0
    safe = jnp.where(held, total, 1.0)
    out_ref[0, 0] = (summed_ref[...] / safe).astype(jnp.bfloat16)
    log_ref[document, pl.ds(head, 1), :] = jnp.where(
        held, highest_ref[...] * scale + jnp.log2(safe), negative
    )


def attend(scale, place, counts, slots, fill, all_rows, pool, keys, values):
    documents, kv_heads, rows, size = all_rows.shape
    blocks, _, _, tokens, _ = pool.shape
    suffix = keys.shape[1]
    group = rows * 2 // suffix
    heads_pad = -(-kv_heads // 8) * 8
    grid_spec = pltpu.PrefetchScalarGridSpec(
        num_scalar_prefetch=4,
        grid=(kv_heads, documents),
        in_specs=[
            pl.BlockSpec((1, 1, rows, size), lambda h, d, *_: (d, h, 0, 0)),
            pl.BlockSpec((blocks, 2, 1, tokens, size), lambda h, d, *_: (0, 0, h, 0, 0)),
            pl.BlockSpec((1, suffix, size), lambda h, d, *_: (h, 0, 0)),
            pl.BlockSpec((1, suffix, size), lambda h, d, *_: (h, 0, 0)),
        ],
        out_specs=[
            pl.BlockSpec((1, 1, size, rows), lambda h, d, *_: (d, h, 0, 0)),
            pl.BlockSpec((documents, heads_pad, rows), lambda h, d, *_: (0, 0, 0)),
        ],
        scratch_shapes=[
            pltpu.VMEM((1, rows), jnp.float32),
            pltpu.VMEM((1, rows), jnp.float32),
            pltpu.VMEM((size, rows), jnp.float32),
        ],
    )
    return pl.pallas_call(
        functools.partial(attend_kernel, scale, group),
        grid_spec=grid_spec,
        out_shape=[
            jax.ShapeDtypeStruct((documents, kv_heads, size, rows), jnp.bfloat16),
            jax.ShapeDtypeStruct((documents, heads_pad, rows), jnp.float32),
        ],
        compiler_params=pltpu.CompilerParams(vmem_limit_bytes=40 * 2**20),
        name="attend",
    )(place, counts, slots, fill, all_rows, pool, keys, values)


def merge_kernel(parts_ref, logs_ref, out_ref):
    documents = parts_ref.shape[0]
    head = pl.program_id(0)
    logs = [logs_ref[o, pl.ds(head, 1), :] for o in range(documents)]
    peak = functools.reduce(jnp.maximum, logs)
    shares = [jnp.exp2(each - peak) for each in logs]
    total = functools.reduce(jnp.add, shares)
    merged = functools.reduce(
        jnp.add,
        [parts_ref[o, 0].astype(jnp.float32) * (shares[o] / total) for o in range(documents)],
    )
    out_ref[0] = merged.T.astype(jnp.bfloat16)


def merge(parts, logs):
    documents, kv_heads, size, rows = parts.shape
    return pl.pallas_call(
        merge_kernel,
        grid=(kv_heads,),
        in_specs=[
            pl.BlockSpec((documents, 1, size, rows), lambda h: (0, h, 0, 0)),
            pl.BlockSpec(logs.shape, lambda h: (0, 0, 0)),
        ],
        out_specs=pl.BlockSpec((1, rows, size), lambda h: (h, 0, 0)),
        out_shape=jax.ShapeDtypeStruct((kv_heads, rows, size), jnp.bfloat16),
        compiler_params=pltpu.CompilerParams(vmem_limit_bytes=40 * 2**20),
        name="merge",
    )(parts, logs)


def to_rows(values, kv_heads):
    count, heads, size = values.shape
    group = heads // kv_heads
    shaped = values.reshape(count, kv_heads, group, size)
    return jnp.transpose(shaped, (1, 0, 2, 3)).reshape(kv_heads, count * group, size)


def from_rows(values, count):
    kv_heads, rows, size = values.shape
    shaped = values.reshape(kv_heads, count, rows // count, size)
    return jnp.transpose(shaped, (1, 0, 2, 3)).reshape(count, kv_heads * (rows // count), size)


def body(queries, new_keys, suffix_values, pool, block_slots, counts, slot_fill):
    local_tokens, _, size = queries.shape
    kv_heads = new_keys.shape[1]
    blocks = pool.shape[0]
    scale = math.log2(math.e) / math.sqrt(size)
    position, replica = lax.axis_index("pool"), lax.axis_index("kvrep")
    place = jnp.stack([position, replica]).astype(jnp.int32)
    own_counts = jnp.take(counts, position, axis=0)
    own_slots = jnp.take(block_slots, position, axis=0)
    own_fill = lax.dynamic_slice_in_dim(slot_fill, position * blocks, blocks)
    suffix = lax.all_gather(jnp.stack([new_keys, suffix_values]), "kvrep", axis=1, tiled=True)
    suffix = jnp.transpose(suffix, (0, 2, 1, 3))
    query_rows = to_rows(queries, kv_heads)
    all_rows = lax.all_gather(query_rows, "pool", axis=0, tiled=False)
    parts, logs = attend(
        scale, place, own_counts, own_slots, own_fill, all_rows, pool, suffix[0], suffix[1]
    )
    parts = lax.all_to_all(parts, "pool", split_axis=0, concat_axis=0, tiled=True)
    logs = lax.all_to_all(logs, "pool", split_axis=0, concat_axis=0, tiled=True)
    return from_rows(merge(parts, logs), local_tokens)


def solution(mesh):
    spread = P(("groups", "pool", "kvrep"), "tp", None)
    placed = (
        spread,
        spread,
        spread,
        P(("groups", "pool"), None, "tp", None, None),
        P("groups", None, None),
        P("groups", None),
        P("groups"),
    )
    return jax.shard_map(
        body, mesh=mesh, in_specs=placed, out_specs=spread, check_vma=False
    )
```

```python
import functools
import math

import jax
import jax.numpy as jnp
from jax import lax
from jax.experimental import pallas as pl
from jax.experimental.pallas import tpu as pltpu
from jax.sharding import PartitionSpec as P

negative = -1e30
NT = (((1,), (1,)), ((), ()))
TN = (((0,), (0,)), ((), ()))


def attend_step(state, key_rows, value_rows, query_rows, scale, allowed):
    highest, total, summed = state
    scores = lax.dot_general(key_rows, query_rows, NT, preferred_element_type=jnp.float32)
    if allowed is not None:
        scores = jnp.where(allowed, scores, negative)
    peak = jnp.maximum(highest, jnp.max(scores, axis=0, keepdims=True))
    weights = jnp.exp2((scores - peak) * scale)
    if allowed is not None:
        weights = jnp.where(allowed, weights, 0.0)
    decay = jnp.exp2((highest - peak) * scale)
    total = total * decay + jnp.sum(weights, axis=0, keepdims=True)
    product = lax.dot_general(
        value_rows, weights.astype(jnp.bfloat16), TN, preferred_element_type=jnp.float32
    )
    return peak, total, summed * decay + product


def suffix_state(h, replica, scale, group, query_ref, keys_ref, values_ref):
    key_rows, query_rows = keys_ref[h], query_ref[h]
    rows, size = query_rows.shape
    shape = (key_rows.shape[0], rows)
    query_pos = replica * (rows // group) + lax.broadcasted_iota(jnp.int32, shape, 1) // group
    allowed = lax.broadcasted_iota(jnp.int32, shape, 0) <= query_pos
    state = (
        jnp.full((1, rows), negative, jnp.float32),
        jnp.zeros((1, rows), jnp.float32),
        jnp.zeros((size, rows), jnp.float32),
    )
    return attend_step(state, key_rows, values_ref[h], query_rows, scale, allowed)


def normalised(highest, total, summed, scale):
    held = total > 0.0
    safe = jnp.where(held, total, 1.0)
    log = jnp.where(held, highest * scale + jnp.log2(safe), negative)
    return summed * (1.0 / safe), log


def fused_kernel(
    owners, kv_heads, scale, group,
    doc_ref, slot_ref, fill_ref, fresh_ref, last_ref,
    query_ref, keys_ref, values_ref, pool_ref, out_ref, *scratch,
):
    gathered = scratch[:kv_heads]
    held_kv = scratch[kv_heads : 2 * kv_heads]
    (
        highest_ref, total_ref, summed_ref, own_log, own_part,
        outbox, outstat, inbox, instat,
        pool_sem, up_send, up_recv, down_send, down_recv,
        part_send, part_recv, stat_send, stat_recv,
    ) = scratch[2 * kv_heads :]
    me, replica = lax.axis_index("pool"), lax.axis_index("kvrep")
    rows, size = query_ref.shape[1:]
    steps = pool_ref.shape[0]
    tokens = pool_ref.shape[3]
    mesh_ids = pl.DeviceIdType.MESH

    loads = [
        pltpu.make_async_copy(pool_ref.at[:, :, h], held_kv[h], pool_sem.at[h])
        for h in range(kv_heads)
    ]
    for load in loads:
        load.start()
    for h in range(kv_heads):
        gathered[h][me] = query_ref[h]

    barrier = pltpu.get_barrier_semaphore()
    for j in range(1, owners):
        pl.semaphore_signal(
            barrier, inc=1, device_id={"pool": lax.rem(me + j, owners)}, device_id_type=mesh_ids
        )
    pl.semaphore_wait(barrier, owners - 1)

    def up(h, k, document):
        return pltpu.make_async_remote_copy(
            src_ref=gathered[h].at[document], dst_ref=gathered[h].at[document],
            send_sem=up_send.at[h, k], recv_sem=up_recv.at[h, k],
            device_id={"pool": me + 1}, device_id_type=mesh_ids,
        )

    def down(h, k, document):
        return pltpu.make_async_remote_copy(
            src_ref=gathered[h].at[document], dst_ref=gathered[h].at[document],
            send_sem=down_send.at[h, k], recv_sem=down_recv.at[h, k],
            device_id={"pool": me - 1}, device_id_type=mesh_ids,
        )

    def sends_up(k):
        return (me - k + 1 >= 0) & (me + 1 < owners)

    def sends_down(k):
        return (me + k - 1 < owners) & (me >= 1)

    def arrive(h, k):
        @pl.when(me - k >= 0)
        def _():
            up(h, k, me - k).wait_recv()

        @pl.when(me + k < owners)
        def _():
            down(h, k, me + k).wait_recv()

    def hop(h, k):
        if k > 1:
            arrive(h, k - 1)

        @pl.when(sends_up(k))
        def _():
            up(h, k, me - k + 1).start()

        @pl.when(sends_down(k))
        def _():
            down(h, k, me + k - 1).start()

    def part_copy(h, j):
        return pltpu.make_async_remote_copy(
            src_ref=outbox.at[h, j], dst_ref=inbox.at[h, j],
            send_sem=part_send.at[h, j], recv_sem=part_recv.at[h, j],
            device_id={"pool": lax.rem(me + j, owners)}, device_id_type=mesh_ids,
        )

    def stat_copy(h, j):
        return pltpu.make_async_remote_copy(
            src_ref=outstat.at[h, j], dst_ref=instat.at[h, j],
            send_sem=stat_send.at[h, j], recv_sem=stat_recv.at[h, j],
            device_id={"pool": lax.rem(me + j, owners)}, device_id_type=mesh_ids,
        )

    waves = [
        [(h, t - h + 1) for h in range(kv_heads) if 1 <= t - h + 1 < owners]
        for t in range(kv_heads + owners - 2)
    ]

    def next_wave():
        if waves:
            for h, k in waves.pop(0):
                hop(h, k)

    def step_at(h):
        def one_step(s, _):
            filled = fill_ref[s]
            slot = slot_ref[s]
            query_rows = gathered[h][doc_ref[s]]
            key_rows, value_rows = held_kv[h][slot, 0], held_kv[h][slot, 1]
            bias = jnp.where(
                lax.broadcasted_iota(jnp.int32, (tokens, 1), 0) < filled, 0.0, negative
            )
            highest = jnp.where(fresh_ref[s] > 0, negative, highest_ref[s])
            scores = bias + lax.dot_general(
                key_rows, query_rows, NT, preferred_element_type=jnp.float32
            )
            peak = jnp.maximum(highest, jnp.max(scores, axis=0, keepdims=True))
            weights = jnp.exp2((scores - peak) * scale)
            decay = jnp.exp2((highest - peak) * scale)
            highest_ref[s + 1] = peak
            total_ref[s + 1] = total_ref[s] * decay + jnp.sum(weights, axis=0, keepdims=True)
            summed_ref[s + 1] = summed_ref[s] * decay + lax.dot_general(
                value_rows, weights.astype(jnp.bfloat16), TN, preferred_element_type=jnp.float32
            )
            return 0

        return one_step

    def state_of(document):
        at = last_ref[document]
        return normalised(highest_ref[at], total_ref[at], summed_ref[at], scale)

    def send_parts(h):
        for j in range(1, owners):
            part, log = state_of(lax.rem(me + j, owners))
            largest = jnp.maximum(jnp.max(jnp.abs(part), axis=0, keepdims=True), 1e-30)
            coded = jnp.round(part * (32767.0 / largest)).astype(jnp.int32).astype(jnp.int16)
            outbox[h, j] = coded
            outstat[h, j, 0:1] = log
            outstat[h, j, 1:2] = largest * (1.0 / 32767.0)
            part_copy(h, j).start()
            stat_copy(h, j).start()

    def own_parts(h):
        part, log = state_of(me)
        suffix_log = own_log[h]
        peak = jnp.maximum(log, suffix_log)
        share, suffix_share = jnp.exp2(log - peak), jnp.exp2(suffix_log - peak)
        total = share + suffix_share
        own_part[h] = part * (share / total) + own_part[h] * (suffix_share / total)
        own_log[h] = peak + jnp.log2(total)

    def merge(h):
        for j in range(1, owners):
            part_copy(h, j).wait_recv()
            stat_copy(h, j).wait_recv()
        logs = [own_log[h]] + [instat[h, j, 0:1] for j in range(1, owners)]
        peak = functools.reduce(jnp.maximum, logs)
        shares = [jnp.exp2(each - peak) for each in logs]
        inverse = 1.0 / functools.reduce(jnp.add, shares)
        merged = own_part[h] * (shares[0] * inverse)
        for j in range(1, owners):
            factor = shares[j] * inverse * instat[h, j, 1:2]
            merged = merged + inbox[h, j].astype(jnp.float32) * factor
        out_ref[h] = merged.T.astype(jnp.bfloat16)

    highest_ref[0] = jnp.full((1, rows), negative, jnp.float32)
    total_ref[0] = jnp.zeros((1, rows), jnp.float32)
    summed_ref[0] = jnp.zeros((size, rows), jnp.float32)

    next_wave()
    for h in range(kv_heads):
        state = suffix_state(h, replica, scale, group, query_ref, keys_ref, values_ref)
        own_part[h], own_log[h] = normalised(*state, scale)
    for _ in range(owners - 2):
        next_wave()
    for h in range(kv_heads):
        loads[h].wait()
        arrive(h, owners - 1)
        lax.fori_loop(0, steps // 2, step_at(h), 0)
        next_wave()
        lax.fori_loop(steps // 2, steps, step_at(h), 0)
        send_parts(h)
        next_wave()
        own_parts(h)
        if h > 0:
            merge(h - 1)
    merge(kv_heads - 1)

    for h in range(kv_heads):
        for k in range(1, owners):
            part_copy(h, k).wait_send()
            stat_copy(h, k).wait_send()

            @pl.when(sends_up(k))
            def _():
                up(h, k, me - k + 1).wait_send()

            @pl.when(sends_down(k))
            def _():
                down(h, k, me + k - 1).wait_send()


def fused(owners, scale, tables, query_rows, keys, values, pool):
    kv_heads, rows, size = query_rows.shape
    blocks, _, _, tokens, _ = pool.shape
    group = rows * 2 // keys.shape[1]
    vmem, smem = pl.BlockSpec(memory_space=pltpu.VMEM), pl.BlockSpec(memory_space=pltpu.SMEM)
    dma = pltpu.SemaphoreType.DMA
    scratch = [pltpu.VMEM((owners, rows, size), jnp.bfloat16)] * kv_heads
    scratch += [pltpu.VMEM((blocks, 2, tokens, size), jnp.bfloat16)] * kv_heads
    scratch += [
        pltpu.VMEM((blocks + 1, 1, rows), jnp.float32),
        pltpu.VMEM((blocks + 1, 1, rows), jnp.float32),
        pltpu.VMEM((blocks + 1, size, rows), jnp.float32),
        pltpu.VMEM((kv_heads, 1, rows), jnp.float32),
        pltpu.VMEM((kv_heads, size, rows), jnp.float32),
        pltpu.VMEM((kv_heads, owners, size, rows), jnp.int16),
        pltpu.VMEM((kv_heads, owners, 2, rows), jnp.float32),
        pltpu.VMEM((kv_heads, owners, size, rows), jnp.int16),
        pltpu.VMEM((kv_heads, owners, 2, rows), jnp.float32),
        dma((kv_heads,)),
    ]
    scratch += [dma((kv_heads, owners))] * 8
    return pl.pallas_call(
        functools.partial(fused_kernel, owners, kv_heads, scale, group),
        in_specs=[smem] * 5 + [vmem] * 3 + [pl.BlockSpec(memory_space=pl.ANY)],
        out_specs=vmem,
        out_shape=jax.ShapeDtypeStruct((kv_heads, rows, size), jnp.bfloat16),
        scratch_shapes=scratch,
        compiler_params=pltpu.CompilerParams(
            collective_id=0, has_side_effects=True, vmem_limit_bytes=56 * 2**20
        ),
        name="fused",
    )(*tables, query_rows, keys, values, pool)


def to_rows(values, kv_heads):
    count, heads, size = values.shape
    group = heads // kv_heads
    shaped = values.reshape(count, kv_heads, group, size)
    return jnp.transpose(shaped, (1, 0, 2, 3)).reshape(kv_heads, count * group, size)


def from_rows(values, count):
    kv_heads, rows, size = values.shape
    shaped = values.reshape(kv_heads, count, rows // count, size)
    return jnp.transpose(shaped, (1, 0, 2, 3)).reshape(count, kv_heads * (rows // count), size)


def step_tables(position, blocks, block_slots, counts, slot_fill):
    own_counts = jnp.take(counts, position, axis=0)
    own_slots = jnp.take(block_slots, position, axis=0)
    own_fill = lax.dynamic_slice_in_dim(slot_fill, position * blocks, blocks)
    ends = jnp.cumsum(own_counts)
    step = jnp.arange(blocks, dtype=jnp.int32)
    ranks = jnp.arange(own_slots.shape[1], dtype=jnp.int32)
    rank = step[:, None] - (ends - own_counts)[None, :]
    held = (rank >= 0) & (step[:, None] < ends[None, :])
    document = jnp.sum(step[:, None] >= ends[None, :], axis=1)
    chosen = held[:, :, None] & (rank[:, :, None] == ranks)
    slot = jnp.sum(jnp.where(chosen, own_slots[None], 0), axis=(1, 2))
    fill = jnp.sum(jnp.where(slot[:, None] == step[None, :], own_fill[None, :], 0), axis=1)
    fresh = jnp.sum(held & (rank == 0), axis=1)
    last = jnp.where(own_counts > 0, ends, 0)
    return [each.astype(jnp.int32) for each in (document, slot, fill, fresh, last)]


def body(queries, new_keys, suffix_values, pool, block_slots, counts, slot_fill):
    local_tokens, _, size = queries.shape
    kv_heads = new_keys.shape[1]
    owners = counts.shape[0]
    scale = math.log2(math.e) / math.sqrt(size)
    position = lax.axis_index("pool")
    tables = step_tables(position, pool.shape[0], block_slots, counts, slot_fill)
    suffix = lax.all_gather(jnp.stack([new_keys, suffix_values]), "kvrep", axis=1, tiled=True)
    suffix = jnp.transpose(suffix, (0, 2, 1, 3))
    query_rows = to_rows(queries, kv_heads)
    attended = fused(owners, scale, tables, query_rows, suffix[0], suffix[1], pool)
    return from_rows(attended, local_tokens)


def solution(mesh):
    spread = P(("groups", "pool", "kvrep"), "tp", None)
    placed = (
        spread,
        spread,
        spread,
        P(("groups", "pool"), None, "tp", None, None),
        P("groups", None, None),
        P("groups", None),
        P("groups"),
    )
    return jax.shard_map(
        body, mesh=mesh, in_specs=placed, out_specs=spread, check_vma=False
    )
```

```python
import functools
import math

import jax
import jax.numpy as jnp
from jax import lax
from jax.experimental import pallas as pl
from jax.experimental.pallas import tpu as pltpu
from jax.sharding import PartitionSpec as P

negative = -1e30
NT = (((1,), (1,)), ((), ()))
TN = (((0,), (0,)), ((), ()))


def attend_step(state, key_rows, value_rows, query_rows, scale, allowed):
    highest, total, summed = state
    scores = lax.dot_general(key_rows, query_rows, NT, preferred_element_type=jnp.float32)
    if allowed is not None:
        scores = jnp.where(allowed, scores, negative)
    peak = jnp.maximum(highest, jnp.max(scores, axis=0, keepdims=True))
    weights = jnp.exp2((scores - peak) * scale)
    if allowed is not None:
        weights = jnp.where(allowed, weights, 0.0)
    decay = jnp.exp2((highest - peak) * scale)
    total = total * decay + jnp.sum(weights, axis=0, keepdims=True)
    product = lax.dot_general(
        value_rows, weights.astype(jnp.bfloat16), TN, preferred_element_type=jnp.float32
    )
    return peak, total, summed * decay + product


def suffix_state(h, replica, scale, group, query_ref, keys_ref, values_ref):
    key_rows, query_rows = keys_ref[h], query_ref[h]
    rows, size = query_rows.shape
    shape = (key_rows.shape[0], rows)
    query_pos = replica * (rows // group) + lax.broadcasted_iota(jnp.int32, shape, 1) // group
    allowed = lax.broadcasted_iota(jnp.int32, shape, 0) <= query_pos
    state = (
        jnp.full((1, rows), negative, jnp.float32),
        jnp.zeros((1, rows), jnp.float32),
        jnp.zeros((size, rows), jnp.float32),
    )
    return attend_step(state, key_rows, values_ref[h], query_rows, scale, allowed)


def normalised(highest, total, summed, scale):
    held = total > 0.0
    safe = jnp.where(held, total, 1.0)
    log = jnp.where(held, highest * scale + jnp.log2(safe), negative)
    return summed * (1.0 / safe), log


def fused_kernel(
    owners, kv_heads, scale, group,
    doc_ref, slot_ref, fill_ref, fresh_ref, last_ref,
    query_ref, keys_ref, values_ref, pool_ref, out_ref, *scratch,
):
    gathered = scratch[:kv_heads]
    held_kv = scratch[kv_heads : 2 * kv_heads]
    (
        highest_ref, total_ref, summed_ref, own_log, own_part,
        outbox, outstat, inbox, instat,
        pool_sem, up_send, up_recv, down_send, down_recv,
        part_send, part_recv, stat_send, stat_recv,
    ) = scratch[2 * kv_heads :]
    me, replica = lax.axis_index("pool"), lax.axis_index("kvrep")
    rows, size = query_ref.shape[1:]
    steps = pool_ref.shape[0]
    tokens = pool_ref.shape[3]
    mesh_ids = pl.DeviceIdType.MESH

    loads = [
        pltpu.make_async_copy(pool_ref.at[:, :, h], held_kv[h], pool_sem.at[h])
        for h in range(kv_heads)
    ]
    for load in loads:
        load.start()
    for h in range(kv_heads):
        gathered[h][me] = query_ref[h]

    barrier = pltpu.get_barrier_semaphore()
    for j in range(1, owners):
        pl.semaphore_signal(
            barrier, inc=1, device_id={"pool": lax.rem(me + j, owners)}, device_id_type=mesh_ids
        )
    pl.semaphore_wait(barrier, owners - 1)

    def up(h, k, document):
        return pltpu.make_async_remote_copy(
            src_ref=gathered[h].at[document], dst_ref=gathered[h].at[document],
            send_sem=up_send.at[h, k], recv_sem=up_recv.at[h, k],
            device_id={"pool": me + 1}, device_id_type=mesh_ids,
        )

    def down(h, k, document):
        return pltpu.make_async_remote_copy(
            src_ref=gathered[h].at[document], dst_ref=gathered[h].at[document],
            send_sem=down_send.at[h, k], recv_sem=down_recv.at[h, k],
            device_id={"pool": me - 1}, device_id_type=mesh_ids,
        )

    def sends_up(k):
        return (me - k + 1 >= 0) & (me + 1 < owners)

    def sends_down(k):
        return (me + k - 1 < owners) & (me >= 1)

    def arrive(h, k):
        @pl.when(me - k >= 0)
        def _():
            up(h, k, me - k).wait_recv()

        @pl.when(me + k < owners)
        def _():
            down(h, k, me + k).wait_recv()

    def hop(h, k):
        if k > 1:
            arrive(h, k - 1)

        @pl.when(sends_up(k))
        def _():
            up(h, k, me - k + 1).start()

        @pl.when(sends_down(k))
        def _():
            down(h, k, me + k - 1).start()

    def part_copies(h, way, j):
        target = {"pool": me + (1, -1)[way]}
        return [
            pltpu.make_async_remote_copy(
                src_ref=source.at[h, way, j], dst_ref=landing.at[h, way, j - 1],
                send_sem=sent.at[h, way, j], recv_sem=received.at[h, way, j - 1],
                device_id=target, device_id_type=mesh_ids,
            )
            for source, landing, sent, received in (
                (outbox, inbox, part_send, part_recv),
                (outstat, instat, stat_send, stat_recv),
            )
        ]

    waves = [
        [(h, t - h + 1) for h in range(kv_heads) if 1 <= t - h + 1 < owners]
        for t in range(kv_heads + owners - 2)
    ]

    def next_wave():
        if waves:
            for h, k in waves.pop(0):
                hop(h, k)

    def step_at(h):
        def one_step(s, _):
            filled = fill_ref[s]
            slot = slot_ref[s]
            query_rows = gathered[h][doc_ref[s]]
            key_rows, value_rows = held_kv[h][slot, 0], held_kv[h][slot, 1]
            bias = jnp.where(
                lax.broadcasted_iota(jnp.int32, (tokens, 1), 0) < filled, 0.0, negative
            )
            highest = jnp.where(fresh_ref[s] > 0, negative, highest_ref[h % 2, s])
            scores = bias + lax.dot_general(
                key_rows, query_rows, NT, preferred_element_type=jnp.float32
            )
            peak = jnp.maximum(highest, jnp.max(scores, axis=0, keepdims=True))
            weights = jnp.exp2((scores - peak) * scale)
            decay = jnp.exp2((highest - peak) * scale)
            highest_ref[h % 2, s + 1] = peak
            total_ref[h % 2, s + 1] = total_ref[h % 2, s] * decay + jnp.sum(
                weights, axis=0, keepdims=True
            )
            summed_ref[h % 2, s + 1] = summed_ref[h % 2, s] * decay + lax.dot_general(
                value_rows, weights.astype(jnp.bfloat16), TN, preferred_element_type=jnp.float32
            )
            return 0

        return one_step

    def state_of(h, document):
        at, held = last_ref[document], h % 2
        return normalised(highest_ref[held, at], total_ref[held, at], summed_ref[held, at], scale)

    def joined(pieces):
        logs = [log for log, _, _ in pieces]
        peak = functools.reduce(jnp.maximum, logs)
        shares = [jnp.exp2(log - peak) for log in logs]
        total = functools.reduce(jnp.add, shares)
        inverse = 1.0 / total
        factors = [
            share * inverse if unit is None else share * inverse * unit
            for share, (_, _, unit) in zip(shares, pieces)
        ]
        part = functools.reduce(
            jnp.add, [part * factor for factor, (_, part, _) in zip(factors, pieces)]
        )
        return part, peak + jnp.log2(total)

    def arrived(h, way, j):
        stats = instat[h, way, j]
        return stats[0:1], inbox[h, way, j].astype(jnp.float32), stats[1:2]

    def pass_on(h, way, j, incoming):
        part, log = state_of(h, me + (j, -j)[way])
        if incoming:
            for copy in part_copies(h, way, j + 1):
                copy.wait_recv()
            part, log = joined([(log, part, None), arrived(h, way, j)])
        largest = jnp.maximum(jnp.max(jnp.abs(part), axis=0, keepdims=True), 1e-30)
        coded = jnp.round(part * (32767.0 / largest)).astype(jnp.int32).astype(jnp.int16)
        outbox[h, way, j] = coded
        outstat[h, way, j, 0:1] = log
        outstat[h, way, j, 1:2] = largest * (1.0 / 32767.0)
        for copy in part_copies(h, way, j):
            copy.start()

    def relay(h, stage, farthest, nearest):
        for way, turn in enumerate((stage - 1, owners - stage)):
            @pl.when(me == turn)
            def _():
                if farthest == nearest:
                    pass_on(h, way, farthest, stage > 1)
                else:
                    def one(i, _):
                        pass_on(h, way, farthest - i, stage > 1)
                        return 0

                    lax.fori_loop(0, farthest - nearest + 1, one, 0)

    def own_parts(h):
        part, log = state_of(h, me)
        own_part[h], own_log[h] = joined([(own_log[h], own_part[h], None), (log, part, None)])

    def finish(h):
        for way, exists in enumerate((me >= 1, me + 1 < owners)):
            @pl.when(exists)
            def _():
                for copy in part_copies(h, way, 1):
                    copy.wait_recv()

        merged, _ = joined(
            [(own_log[h], own_part[h], None), arrived(h, 0, 0), arrived(h, 1, 0)]
        )
        out_ref[h] = merged.T.astype(jnp.bfloat16)

    for held in range(2):
        highest_ref[held, 0] = jnp.full((1, rows), negative, jnp.float32)
        total_ref[held, 0] = jnp.zeros((1, rows), jnp.float32)
        summed_ref[held, 0] = jnp.zeros((size, rows), jnp.float32)
    for way, missing in enumerate((me < 1, me + 1 >= owners)):
        @pl.when(missing)
        def _():
            for h in range(kv_heads):
                inbox[h, way, 0] = jnp.zeros((size, rows), jnp.int16)
                instat[h, way, 0, 0:1] = jnp.full((1, rows), negative, jnp.float32)
                instat[h, way, 0, 1:2] = jnp.zeros((1, rows), jnp.float32)

    next_wave()
    for h in range(kv_heads):
        state = suffix_state(h, replica, scale, group, query_ref, keys_ref, values_ref)
        own_part[h], own_log[h] = normalised(*state, scale)
    for _ in range(owners - 2):
        next_wave()

    quarters = 4
    events = {}

    def plan(slot, act, *args):
        events.setdefault(slot, []).append(functools.partial(act, *args))

    for h in range(kv_heads):
        done = quarters * (h + 1)
        plan(done, relay, h, 1, owners - 1, 1)
        plan(done, own_parts, h)
    for i in range(len(waves)):
        plan(2 + 2 * i, next_wave)
    for h in range(kv_heads):
        done = quarters * (h + 1)
        for stage in range(2, owners):
            farthest = owners - stage
            if stage == 2:
                plan(done + 2, relay, h, stage, farthest, farthest)
                if farthest > 1:
                    plan(done + 3, relay, h, stage, farthest - 1, 1)
            else:
                plan(done + 4, relay, h, stage, farthest, 1)
        plan(done + 7, finish, h)

    for slot in range(quarters * (kv_heads + 1) + 4):
        for act in events.get(slot, []):
            act()
        h, quarter = divmod(slot, quarters)
        if h < kv_heads:
            if quarter == 0:
                loads[h].wait()
                arrive(h, owners - 1)
            first, end = steps * quarter // quarters, steps * (quarter + 1) // quarters
            lax.fori_loop(first, end, step_at(h), 0)

    for h in range(kv_heads):
        for k in range(1, owners):
            for way, sends in enumerate((me + k < owners, me - k >= 0)):
                @pl.when(sends)
                def _():
                    for copy in part_copies(h, way, k):
                        copy.wait_send()

            @pl.when(sends_up(k))
            def _():
                up(h, k, me - k + 1).wait_send()

            @pl.when(sends_down(k))
            def _():
                down(h, k, me + k - 1).wait_send()


def fused(owners, scale, tables, query_rows, keys, values, pool):
    kv_heads, rows, size = query_rows.shape
    blocks, _, _, tokens, _ = pool.shape
    group = rows * 2 // keys.shape[1]
    vmem, smem = pl.BlockSpec(memory_space=pltpu.VMEM), pl.BlockSpec(memory_space=pltpu.SMEM)
    dma = pltpu.SemaphoreType.DMA
    scratch = [pltpu.VMEM((owners, rows, size), jnp.bfloat16)] * kv_heads
    scratch += [pltpu.VMEM((blocks, 2, tokens, size), jnp.bfloat16)] * kv_heads
    scratch += [
        pltpu.VMEM((2, blocks + 1, 1, rows), jnp.float32),
        pltpu.VMEM((2, blocks + 1, 1, rows), jnp.float32),
        pltpu.VMEM((2, blocks + 1, size, rows), jnp.float32),
        pltpu.VMEM((kv_heads, 1, rows), jnp.float32),
        pltpu.VMEM((kv_heads, size, rows), jnp.float32),
        pltpu.VMEM((kv_heads, 2, owners, size, rows), jnp.int16),
        pltpu.VMEM((kv_heads, 2, owners, 2, rows), jnp.float32),
        pltpu.VMEM((kv_heads, 2, owners, size, rows), jnp.int16),
        pltpu.VMEM((kv_heads, 2, owners, 2, rows), jnp.float32),
        dma((kv_heads,)),
    ]
    scratch += [dma((kv_heads, owners))] * 4 + [dma((kv_heads, 2, owners))] * 4
    return pl.pallas_call(
        functools.partial(fused_kernel, owners, kv_heads, scale, group),
        in_specs=[smem] * 5 + [vmem] * 3 + [pl.BlockSpec(memory_space=pl.ANY)],
        out_specs=vmem,
        out_shape=jax.ShapeDtypeStruct((kv_heads, rows, size), jnp.bfloat16),
        scratch_shapes=scratch,
        compiler_params=pltpu.CompilerParams(
            collective_id=0, has_side_effects=True, vmem_limit_bytes=60 * 2**20
        ),
        name="fused",
    )(*tables, query_rows, keys, values, pool)


def to_rows(values, kv_heads):
    count, heads, size = values.shape
    group = heads // kv_heads
    shaped = values.reshape(count, kv_heads, group, size)
    return jnp.transpose(shaped, (1, 0, 2, 3)).reshape(kv_heads, count * group, size)


def from_rows(values, count):
    kv_heads, rows, size = values.shape
    shaped = values.reshape(kv_heads, count, rows // count, size)
    return jnp.transpose(shaped, (1, 0, 2, 3)).reshape(count, kv_heads * (rows // count), size)


def step_tables(position, blocks, block_slots, counts, slot_fill):
    own_counts = jnp.take(counts, position, axis=0)
    own_slots = jnp.take(block_slots, position, axis=0)
    own_fill = lax.dynamic_slice_in_dim(slot_fill, position * blocks, blocks)
    ends = jnp.cumsum(own_counts)
    step = jnp.arange(blocks, dtype=jnp.int32)
    ranks = jnp.arange(own_slots.shape[1], dtype=jnp.int32)
    rank = step[:, None] - (ends - own_counts)[None, :]
    held = (rank >= 0) & (step[:, None] < ends[None, :])
    document = jnp.sum(step[:, None] >= ends[None, :], axis=1)
    chosen = held[:, :, None] & (rank[:, :, None] == ranks)
    slot = jnp.sum(jnp.where(chosen, own_slots[None], 0), axis=(1, 2))
    fill = jnp.sum(jnp.where(slot[:, None] == step[None, :], own_fill[None, :], 0), axis=1)
    fresh = jnp.sum(held & (rank == 0), axis=1)
    last = jnp.where(own_counts > 0, ends, 0)
    return [each.astype(jnp.int32) for each in (document, slot, fill, fresh, last)]


def body(queries, new_keys, suffix_values, pool, block_slots, counts, slot_fill):
    local_tokens, _, size = queries.shape
    kv_heads = new_keys.shape[1]
    owners = counts.shape[0]
    scale = math.log2(math.e) / math.sqrt(size)
    position = lax.axis_index("pool")
    tables = step_tables(position, pool.shape[0], block_slots, counts, slot_fill)
    suffix = lax.all_gather(jnp.stack([new_keys, suffix_values]), "kvrep", axis=1, tiled=True)
    suffix = jnp.transpose(suffix, (0, 2, 1, 3))
    query_rows = to_rows(queries, kv_heads)
    attended = fused(owners, scale, tables, query_rows, suffix[0], suffix[1], pool)
    return from_rows(attended, local_tokens)


def solution(mesh):
    spread = P(("groups", "pool", "kvrep"), "tp", None)
    placed = (
        spread,
        spread,
        spread,
        P(("groups", "pool"), None, "tp", None, None),
        P("groups", None, None),
        P("groups", None),
        P("groups"),
    )
    return jax.shard_map(
        body, mesh=mesh, in_specs=placed, out_specs=spread, check_vma=False
    )
```

```python
import functools
import math

import jax
import jax.numpy as jnp
from jax import lax
from jax.experimental import pallas as pl
from jax.experimental.pallas import tpu as pltpu
from jax.sharding import PartitionSpec as P

negative = -1e30
NT = (((1,), (1,)), ((), ()))
TN = (((0,), (0,)), ((), ()))


def attend_step(state, key_rows, value_rows, query_rows, scale, allowed):
    highest, total, summed = state
    scores = lax.dot_general(key_rows, query_rows, NT, preferred_element_type=jnp.float32)
    if allowed is not None:
        scores = jnp.where(allowed, scores, negative)
    peak = jnp.maximum(highest, jnp.max(scores, axis=0, keepdims=True))
    weights = jnp.exp2((scores - peak) * scale)
    if allowed is not None:
        weights = jnp.where(allowed, weights, 0.0)
    decay = jnp.exp2((highest - peak) * scale)
    total = total * decay + jnp.sum(weights, axis=0, keepdims=True)
    product = lax.dot_general(
        value_rows, weights.astype(jnp.bfloat16), TN, preferred_element_type=jnp.float32
    )
    return peak, total, summed * decay + product


def suffix_state(h, replica, scale, group, query_ref, keys_ref, values_ref):
    key_rows, query_rows = keys_ref[h], query_ref[h]
    rows, size = query_rows.shape
    shape = (key_rows.shape[0], rows)
    query_pos = replica * (rows // group) + lax.broadcasted_iota(jnp.int32, shape, 1) // group
    allowed = lax.broadcasted_iota(jnp.int32, shape, 0) <= query_pos
    state = (
        jnp.full((1, rows), negative, jnp.float32),
        jnp.zeros((1, rows), jnp.float32),
        jnp.zeros((size, rows), jnp.float32),
    )
    return attend_step(state, key_rows, values_ref[h], query_rows, scale, allowed)


def normalised(highest, total, summed, scale):
    held = total > 0.0
    safe = jnp.where(held, total, 1.0)
    log = jnp.where(held, highest * scale + jnp.log2(safe), negative)
    return summed * (1.0 / safe), log


def fused_kernel(
    owners, kv_heads, scale, group,
    counts_ref, slots_ref, fill_ref,
    query_ref, keys_ref, values_ref, pool_ref, out_ref, *scratch,
):
    gathered = scratch[:kv_heads]
    held_kv = scratch[kv_heads : 2 * kv_heads]
    (
        highest_ref, total_ref, summed_ref, own_log, own_part,
        outbox, outstat, inbox, instat,
        pool_sem, query_send, query_recv,
        part_send, part_recv, stat_send, stat_recv,
    ) = scratch[2 * kv_heads :]
    me, replica = lax.axis_index("pool"), lax.axis_index("kvrep")
    rows, size = query_ref.shape[1:]
    steps = pool_ref.shape[0]
    tokens = pool_ref.shape[3]
    mesh_ids = pl.DeviceIdType.MESH

    loads = [
        pltpu.make_async_copy(pool_ref.at[:, :, h], held_kv[h], pool_sem.at[h])
        for h in range(kv_heads)
    ]
    for load in loads:
        load.start()
    for h in range(kv_heads):
        gathered[h][me] = query_ref[h]

    barrier = pltpu.get_barrier_semaphore()
    for j in range(1, owners):
        pl.semaphore_signal(
            barrier, inc=1, device_id={"pool": lax.rem(me + j, owners)}, device_id_type=mesh_ids
        )
    pl.semaphore_wait(barrier, owners - 1)

    def query_copy(h, way, k, document):
        sign = (1, -1)[way]
        return pltpu.make_async_remote_copy(
            src_ref=gathered[h].at[document], dst_ref=gathered[h].at[document],
            send_sem=query_send.at[h, way, k], recv_sem=query_recv.at[h, way, k],
            device_id={"pool": me + sign * (2 if k == 2 else 1)}, device_id_type=mesh_ids,
        )

    def if_sends(way, k, act):
        sign = (1, -1)[way]
        target = me + sign * (2 if k == 2 else 1)
        source = me - sign * (k - 1 if k > 2 else 0)

        @pl.when((target >= 0) & (target < owners) & (source >= 0) & (source < owners))
        def _():
            act(source)

    def send_queries(h, k):
        for way in range(2):
            if_sends(way, k, lambda source: query_copy(h, way, k, source).start())

    def arrive(h, k):
        @pl.when(me - k >= 0)
        def _():
            query_copy(h, 0, k, me - k).wait_recv()

        @pl.when(me + k < owners)
        def _():
            query_copy(h, 1, k, me + k).wait_recv()

    def issue(h):
        for k in range(1, min(3, owners)):
            send_queries(h, k)

    def forward(h):
        for k in range(3, owners):
            arrive(h, k - 1)
            send_queries(h, k)

    def part_copies(h, way, j):
        target = {"pool": me + (1, -1)[way]}
        return [
            pltpu.make_async_remote_copy(
                src_ref=source.at[h, way, j], dst_ref=landing.at[h, way, j - 1],
                send_sem=sent.at[h, way, j], recv_sem=received.at[h, way, j - 1],
                device_id=target, device_id_type=mesh_ids,
            )
            for source, landing, sent, received in (
                (outbox, inbox, part_send, part_recv),
                (outstat, instat, stat_send, stat_recv),
            )
        ]

    capacity = slots_ref.shape[0] // (owners * owners)

    def step_place(s):
        document, first, end = 0, 0, 0
        for each in range(owners):
            end = end + counts_ref[me * owners + each]
            past = s >= end
            document = jnp.where(past, each + 1, document)
            first = jnp.where(past, end, first)
        return jnp.minimum(document, owners - 1), jnp.minimum(s - first, capacity - 1)

    def last_step(document):
        end, last = 0, 0
        for each in range(owners):
            held = counts_ref[me * owners + each]
            end = end + held
            last = jnp.where((document == each) & (held > 0), end, last)
        return last

    def step_at(h):
        def one_step(s, _):
            document, rank = step_place(s)
            slot = slots_ref[(me * owners + document) * capacity + rank]
            filled = fill_ref[me * steps + slot]
            key_rows, value_rows = held_kv[h][slot, 0], held_kv[h][slot, 1]
            bias = jnp.where(
                lax.broadcasted_iota(jnp.int32, (tokens, 1), 0) < filled, 0.0, negative
            )
            fresh = rank == 0
            scores = bias + lax.dot_general(
                key_rows, gathered[h][document], NT, preferred_element_type=jnp.float32
            )
            highest = jnp.where(fresh, negative, highest_ref[h % 2, s])
            peak = jnp.maximum(highest, jnp.max(scores, axis=0, keepdims=True))
            weights = jnp.exp2((scores - peak) * scale)
            decay = jnp.exp2((highest - peak) * scale)
            highest_ref[h % 2, s + 1] = peak
            total_ref[h % 2, s + 1] = total_ref[h % 2, s] * decay + jnp.sum(
                weights, axis=0, keepdims=True
            )
            summed_ref[h % 2, s + 1] = summed_ref[h % 2, s] * decay + lax.dot_general(
                value_rows, weights.astype(jnp.bfloat16), TN, preferred_element_type=jnp.float32
            )
            return 0

        return one_step

    def state_of(h, document):
        at, held = last_step(document), h % 2
        return normalised(highest_ref[held, at], total_ref[held, at], summed_ref[held, at], scale)

    def joined(pieces):
        logs = [log for log, _, _ in pieces]
        peak = functools.reduce(jnp.maximum, logs)
        shares = [jnp.exp2(log - peak) for log in logs]
        total = functools.reduce(jnp.add, shares)
        inverse = 1.0 / total
        factors = [
            share * inverse if unit is None else share * inverse * unit
            for share, (_, _, unit) in zip(shares, pieces)
        ]
        part = functools.reduce(
            jnp.add, [part * factor for factor, (_, part, _) in zip(factors, pieces)]
        )
        return part, peak + jnp.log2(total)

    def arrived(h, way, j):
        stats = instat[h, way, j]
        return stats[0:1], inbox[h, way, j].astype(jnp.float32), stats[1:2]

    def pass_on(h, way, j, incoming):
        part, log = state_of(h, me + (j, -j)[way])
        if incoming:
            for copy in part_copies(h, way, j + 1):
                copy.wait_recv()
            part, log = joined([(log, part, None), arrived(h, way, j)])
        largest = jnp.maximum(jnp.max(jnp.abs(part), axis=0, keepdims=True), 1e-30)
        coded = jnp.round(part * (32767.0 / largest)).astype(jnp.int32).astype(jnp.int16)
        outbox[h, way, j] = coded
        outstat[h, way, j, 0:1] = log
        outstat[h, way, j, 1:2] = largest * (1.0 / 32767.0)
        for copy in part_copies(h, way, j):
            copy.start()

    def relay(h, stage, farthest, nearest):
        for way, turn in enumerate((stage - 1, owners - stage)):
            @pl.when(me == turn)
            def _():
                if farthest == nearest:
                    pass_on(h, way, farthest, stage > 1)
                else:
                    def one(i, _):
                        pass_on(h, way, farthest - i, stage > 1)
                        return 0

                    lax.fori_loop(0, farthest - nearest + 1, one, 0)

    def own_parts(h):
        part, log = state_of(h, me)
        own_part[h], own_log[h] = joined([(own_log[h], own_part[h], None), (log, part, None)])

    def finish(h):
        for way, exists in enumerate((me >= 1, me + 1 < owners)):
            @pl.when(exists)
            def _():
                for copy in part_copies(h, way, 1):
                    copy.wait_recv()

        merged, _ = joined(
            [(own_log[h], own_part[h], None), arrived(h, 0, 0), arrived(h, 1, 0)]
        )
        out_ref[h] = merged.T.astype(jnp.bfloat16)

    for held in range(2):
        highest_ref[held, 0] = jnp.full((1, rows), negative, jnp.float32)
        total_ref[held, 0] = jnp.zeros((1, rows), jnp.float32)
        summed_ref[held, 0] = jnp.zeros((size, rows), jnp.float32)
    for way, missing in enumerate((me < 1, me + 1 >= owners)):
        @pl.when(missing)
        def _():
            for h in range(kv_heads):
                inbox[h, way, 0] = jnp.zeros((size, rows), jnp.int16)
                instat[h, way, 0, 0:1] = jnp.full((1, rows), negative, jnp.float32)
                instat[h, way, 0, 1:2] = jnp.zeros((1, rows), jnp.float32)

    def suffix_part(h):
        state = suffix_state(h, replica, scale, group, query_ref, keys_ref, values_ref)
        own_part[h], own_log[h] = normalised(*state, scale)

    FWD = 2
    FIRST = kv_heads
    for h in range(FIRST):
        issue(h)
    for h in range(kv_heads):
        if h == min(1, kv_heads - 1):
            forward(0)
            for later in range(FIRST, kv_heads):
                issue(later)
        suffix_part(h)

    quarters = 4
    events = {}

    def plan(slot, act, *args):
        events.setdefault(slot, []).append(functools.partial(act, *args))

    for h in range(kv_heads):
        done = quarters * (h + 1)
        plan(done, relay, h, 1, owners - 1, 1)
        plan(done, own_parts, h)
    for h in range(kv_heads):
        if h + 1 < kv_heads:
            plan(quarters * h + FWD, forward, h + 1)
    for h in range(kv_heads):
        done = quarters * (h + 1)
        for stage in range(2, owners):
            farthest = owners - stage
            if stage == 2:
                plan(done + 2, relay, h, stage, farthest, farthest)
                if farthest > 1:
                    plan(done + 3, relay, h, stage, farthest - 1, 1)
            else:
                plan(done + 4, relay, h, stage, farthest, 1)
        plan(done + 7, finish, h)

    for slot in range(quarters * (kv_heads + 1) + 4):
        for act in events.get(slot, []):
            act()
        h, quarter = divmod(slot, quarters)
        if h < kv_heads:
            if quarter == 0:
                loads[h].wait()
                for k in sorted({1, owners - 1}):
                    arrive(h, k)
            first, end = steps * quarter // quarters, steps * (quarter + 1) // quarters
            lax.fori_loop(first, end, step_at(h), 0)

    for h in range(kv_heads):
        for k in range(1, owners):
            for way, sends in enumerate((me + k < owners, me - k >= 0)):
                @pl.when(sends)
                def _():
                    for copy in part_copies(h, way, k):
                        copy.wait_send()

            for way in range(2):
                if_sends(way, k, lambda source: query_copy(h, way, k, source).wait_send())


def fused(owners, scale, tables, query_rows, keys, values, pool):
    kv_heads, rows, size = query_rows.shape
    blocks, _, _, tokens, _ = pool.shape
    group = rows * 2 // keys.shape[1]
    vmem, smem = pl.BlockSpec(memory_space=pltpu.VMEM), pl.BlockSpec(memory_space=pltpu.SMEM)
    dma = pltpu.SemaphoreType.DMA
    scratch = [pltpu.VMEM((owners, rows, size), jnp.bfloat16)] * kv_heads
    scratch += [pltpu.VMEM((blocks, 2, tokens, size), jnp.bfloat16)] * kv_heads
    scratch += [
        pltpu.VMEM((2, blocks + 1, 1, rows), jnp.float32),
        pltpu.VMEM((2, blocks + 1, 1, rows), jnp.float32),
        pltpu.VMEM((2, blocks + 1, size, rows), jnp.float32),
        pltpu.VMEM((kv_heads, 1, rows), jnp.float32),
        pltpu.VMEM((kv_heads, size, rows), jnp.float32),
        pltpu.VMEM((kv_heads, 2, owners, size, rows), jnp.int16),
        pltpu.VMEM((kv_heads, 2, owners, 2, rows), jnp.float32),
        pltpu.VMEM((kv_heads, 2, owners, size, rows), jnp.int16),
        pltpu.VMEM((kv_heads, 2, owners, 2, rows), jnp.float32),
        dma((kv_heads,)),
    ]
    scratch += [dma((kv_heads, 2, owners))] * 6
    return pl.pallas_call(
        functools.partial(fused_kernel, owners, kv_heads, scale, group),
        in_specs=[smem] * 3 + [vmem] * 3 + [pl.BlockSpec(memory_space=pl.ANY)],
        out_specs=vmem,
        out_shape=jax.ShapeDtypeStruct((kv_heads, rows, size), jnp.bfloat16),
        scratch_shapes=scratch,
        compiler_params=pltpu.CompilerParams(
            collective_id=0, has_side_effects=True, vmem_limit_bytes=60 * 2**20
        ),
        name="fused",
    )(*tables, query_rows, keys, values, pool)


def to_rows(values, kv_heads):
    count, heads, size = values.shape
    group = heads // kv_heads
    shaped = values.reshape(count, kv_heads, group, size)
    return jnp.transpose(shaped, (1, 0, 2, 3)).reshape(kv_heads, count * group, size)


def from_rows(values, count):
    kv_heads, rows, size = values.shape
    shaped = values.reshape(kv_heads, count, rows // count, size)
    return jnp.transpose(shaped, (1, 0, 2, 3)).reshape(count, kv_heads * (rows // count), size)


def body(queries, new_keys, suffix_values, pool, block_slots, counts, slot_fill):
    local_tokens, _, size = queries.shape
    kv_heads = new_keys.shape[1]
    owners = counts.shape[0]
    scale = math.log2(math.e) / math.sqrt(size)
    tables = [counts.reshape(-1), block_slots.reshape(-1), slot_fill]
    suffix = lax.all_gather(jnp.stack([new_keys, suffix_values]), "kvrep", axis=1, tiled=True)
    suffix = jnp.transpose(suffix, (0, 2, 1, 3))
    query_rows = to_rows(queries, kv_heads)
    attended = fused(owners, scale, tables, query_rows, suffix[0], suffix[1], pool)
    return from_rows(attended, local_tokens)


def solution(mesh):
    spread = P(("groups", "pool", "kvrep"), "tp", None)
    placed = (
        spread,
        spread,
        spread,
        P(("groups", "pool"), None, "tp", None, None),
        P("groups", None, None),
        P("groups", None),
        P("groups"),
    )
    return jax.shard_map(
        body, mesh=mesh, in_specs=placed, out_specs=spread, check_vma=False
    )
```
